32 devices in a mesh: seq: 16 (over z, y, core), fsdp: 2 (over x).
Axes of the slice: x: 2, y: 2, z: 4, core: 2. Of those that a mesh axis runs over, the one named last changes fastest.
Arguments:
- inputs: bfloat16 [4, 4096, 1536], P('fsdp', 'seq'), may hold values from -6 to 6
- gain: float32 [1536], replicated, may hold values from 0.1 to 1.9
- param: bfloat16 [1536, 3, 1536], P('fsdp'), may hold values from -6 to 6
- cotangent: bfloat16 [4, 4096, 1536], P('fsdp', 'seq'), may hold values from -12 to 12
- noise: bfloat16 [1536, 3, 1536], P('fsdp'), may hold values from -6 to 6
Outputs:
- outputs: bfloat16 [4, 4096, 1536], P('fsdp', 'seq')
- new_param: bfloat16 [1536, 3, 1536], P('fsdp')
The draws below stay inside these ranges and needn't reach their ends.
All inputs are finite; a program needn't handle non-finite values.
Results may differ from the reference program's by a relative error of at most 0.012.
Values may be sent and summed in bfloat16 or wider, within the bound.
A program may use at most 128 MiB of HBM per device.

```python
import math
import jax
import jax.numpy as jnp
from jax import lax

CHANNEL_COUNT = 1536
SEQUENCE_LENGTH = 4096
DILATION_STEP = 16
SEQUENCES_SHARD = 2
BATCH = 4
POSITIONS_SHARD = 256
N_SEQ = 16
N_FSDP = 2


def draw_cotangent(key, part):
    key = jax.random.fold_in(key, 7)
    value_key = jax.random.fold_in(key, 0)
    pair_key = jax.random.fold_in(key, 2)
    shape = (BATCH, SEQUENCE_LENGTH, CHANNEL_COUNT)
    values = jax.random.truncated_normal(value_key, -3.0, 3.0, shape, jnp.float32)
    block_count = BATCH // SEQUENCES_SHARD
    pairing = jax.random.permutation(pair_key, block_count)
    batch_block = jnp.arange(BATCH) // SEQUENCES_SHARD
    channel_block = jnp.arange(CHANNEL_COUNT) // (CHANNEL_COUNT // block_count)
    chosen = pairing[batch_block][:, None] == channel_block[None, :]
    factor = jnp.where(chosen, 3.0, 1.0).astype(jnp.float32)
    return (values * factor[:, None, :]).astype(jnp.bfloat16)


def block_levels(stream_key, shape, pieces, smallest, high):
    loudness, own = 1.0, jax.random.fold_in(stream_key, 6)
    for axis_at, blocks in pieces:
        heights = jnp.exp(jax.random.uniform(jax.random.fold_in(own, axis_at), (blocks,), jnp.float32, smallest / len(pieces), high / len(pieces)))
        loudness = loudness * jnp.repeat(heights, shape[axis_at] // blocks).reshape([-1 if axis == axis_at else 1 for axis in range(len(shape))])
    return loudness


def centred(stream_key, dims, spread, limit, cuts=(), kind=jnp.bfloat16):
    result = jax.random.normal(stream_key, dims, jnp.float32) * spread
    if len(cuts) > 0:
        result = block_levels(stream_key, dims, cuts, -0.22, 0.18) * result
    return jnp.clip(result, min=-limit, max=limit).astype(kind)


def setup_inputs(seed: int = 0) -> dict:
    splits = jax.random.split(jax.random.key(seed), 6)
    return {
        "inputs": centred(splits[0], (BATCH, SEQUENCE_LENGTH, CHANNEL_COUNT), 1.0, 6.0, ((0, 2), (1, 16))),
        "gain": jnp.clip(1.0 + 0.18 * jax.random.normal(splits[1], (CHANNEL_COUNT,), jnp.float32), 0.1, 1.9),
        "param": centred(splits[2], (CHANNEL_COUNT, 3, CHANNEL_COUNT), 1.0, 6.0, ((0, 2),)),
        "cotangent": draw_cotangent(jax.random.fold_in(splits[5], 71), 0),
        "noise": centred(splits[4], (CHANNEL_COUNT, 3, CHANNEL_COUNT), 1.0, 6.0, ((0, 2),)),
    }


def normalise(values, gain):
    floats = values.astype(jnp.float32)
    factor = lax.rsqrt(lax.optimization_barrier(jnp.mean(floats * floats, axis=-1, keepdims=True)) + 1e-06)
    return jax.nn.gelu(floats * factor * gain).astype(jnp.bfloat16)

def reference(inputs, gain, param, cotangent, noise):
    scale = 1.0 / math.sqrt(3.0 * CHANNEL_COUNT)
    hidden_state = normalise(inputs, gain)
    padded_input = jnp.pad(hidden_state, ((0, 0), (DILATION_STEP, DILATION_STEP), (0, 0)))

    def forward_one(sequence_index):
        total = jnp.zeros((SEQUENCE_LENGTH, CHANNEL_COUNT), jnp.float32)
        for kernel_tap in range(3):
            input_window = sequence_index[kernel_tap * DILATION_STEP:kernel_tap * DILATION_STEP + SEQUENCE_LENGTH, :]
            total = total + jnp.dot(input_window, param[:, kernel_tap, :].T, preferred_element_type=jnp.float32)
        return total * scale
    mixed = lax.map(forward_one, padded_input)
    outputs = (inputs.astype(jnp.float32) + mixed).astype(jnp.bfloat16)
    zeroed_index = jnp.zeros((), jnp.int32)

    def add_block(index, total):
        index = jnp.asarray(index).astype(jnp.int32)
        row_tile = index // N_SEQ
        position_block = index % N_SEQ
        hidden_tile = lax.dynamic_slice(padded_input, (row_tile * SEQUENCES_SHARD, position_block * POSITIONS_SHARD, zeroed_index), (SEQUENCES_SHARD, POSITIONS_SHARD + 2 * DILATION_STEP, CHANNEL_COUNT))
        grad_block = lax.dynamic_slice(cotangent, (row_tile * SEQUENCES_SHARD, position_block * POSITIONS_SHARD, zeroed_index), (SEQUENCES_SHARD, POSITIONS_SHARD, CHANNEL_COUNT))
        flat_grad = grad_block.reshape(SEQUENCES_SHARD * POSITIONS_SHARD, CHANNEL_COUNT)
        taps = []
        for kernel_tap in range(3):
            input_window = hidden_tile[:, kernel_tap * DILATION_STEP:kernel_tap * DILATION_STEP + POSITIONS_SHARD, :].reshape(SEQUENCES_SHARD * POSITIONS_SHARD, CHANNEL_COUNT)
            taps.append(jnp.dot(flat_grad.T, input_window, preferred_element_type=jnp.float32))
        term = (jnp.stack(taps, axis=1) * scale).astype(jnp.bfloat16)
        term = lax.optimization_barrier(term)
        return total + term.astype(jnp.float32)
    grad = lax.fori_loop(0, N_FSDP * N_SEQ, add_block, jnp.zeros((CHANNEL_COUNT, 3, CHANNEL_COUNT), jnp.float32))
    eta = math.sqrt(3.0 * CHANNEL_COUNT / (BATCH * SEQUENCE_LENGTH))
    updated = param.astype(jnp.float32) - eta * grad + math.sqrt(2.0 * eta) * noise.astype(jnp.float32)
    return (outputs, updated.astype(jnp.bfloat16))
```

```python
import functools
import math

import jax
import jax.numpy as jnp
from jax import lax
from jax.experimental import pallas as pl
from jax.experimental.pallas import tpu as pltpu
from jax.sharding import PartitionSpec as P

DILATION_STEP = 16
MESH = pl.DeviceIdType.MESH
F32 = jnp.float32
BF16 = jnp.bfloat16


def padded(x, sides, width):
    for axis, dim in sides:
        count, length = (lax.axis_size(axis), x.shape[dim])
        up = [(i, (i + 1) % count) for i in range(count - 1)]
        down = [(j, i) for i, j in up]
        last = lax.slice_in_dim(x, length - width, length, axis=dim)
        first = lax.slice_in_dim(x, 0, width, axis=dim)
        before = lax.ppermute(last, axis, up)
        after = lax.ppermute(first, axis, down)
        x = jnp.concatenate([before, x, after], axis=dim)
    return x


def normalise(values, gain):
    floats = values.astype(jnp.float32)
    factor = lax.rsqrt(jnp.mean(floats * floats, axis=-1, keepdims=True) + 1e-06)
    return jax.nn.gelu(floats * factor * gain).astype(jnp.bfloat16)


def convolve(source_rows, kernel, scale):
    span_length = source_rows.shape[1] - 2 * DILATION_STEP
    total = jnp.zeros((source_rows.shape[0], span_length, kernel.shape[0]), jnp.float32)
    for kernel_tap in range(3):
        input_window = source_rows[
            :, kernel_tap * DILATION_STEP : kernel_tap * DILATION_STEP + span_length, :
        ]
        total = total + lax.dot_general(
            input_window,
            kernel[:, kernel_tap, :],
            (((2,), (1,)), ((), ())),
            preferred_element_type=jnp.float32,
        )
    return total * scale


def shards(inputs, gain, param, cotangent, noise):
    seqs, span_length, width = inputs.shape
    scale = 1.0 / math.sqrt(3.0 * width)
    total_rows = seqs * lax.axis_size("fsdp") * span_length * lax.axis_size("seq")
    eta = math.sqrt(3.0 * width / total_rows)
    hidden_state = normalise(inputs, gain)
    padded_input = padded(hidden_state, (("seq", 1),), DILATION_STEP)
    mixed = convolve(padded_input, lax.all_gather(param, "fsdp", axis=0, tiled=True), scale)
    taps = []
    for kernel_tap in range(3):
        input_window = padded_input[
            :, kernel_tap * DILATION_STEP : kernel_tap * DILATION_STEP + span_length, :
        ]
        taps.append(
            lax.dot_general(
                cotangent,
                input_window,
                (((0, 1), (0, 1)), ((), ())),
                preferred_element_type=jnp.float32,
            )
        )
    term = (jnp.stack(taps, axis=1) * scale).astype(jnp.bfloat16)
    term = lax.optimization_barrier(term)
    share = lax.psum_scatter(
        term.astype(jnp.float32).astype(jnp.bfloat16), "fsdp", scatter_dimension=0, tiled=True
    ).astype(jnp.float32)
    seq_share = lax.psum_scatter(share, "seq", scatter_dimension=0, tiled=True)
    piece_rows = seq_share.shape[0]
    offset = lax.axis_index("seq") * piece_rows
    own_param = lax.dynamic_slice_in_dim(param, offset, piece_rows, 0)
    own_noise = lax.dynamic_slice_in_dim(noise, offset, piece_rows, 0)
    updated = (
        own_param.astype(jnp.float32)
        - eta * seq_share
        + math.sqrt(2.0 * eta) * own_noise.astype(jnp.float32)
    )
    new_param = lax.all_gather(updated.astype(jnp.bfloat16), "seq", axis=0, tiled=True)
    outputs = (inputs.astype(jnp.float32) + mixed).astype(jnp.bfloat16)
    return (outputs, new_param)


def ring_kernel(
    ring,
    scale,
    eta,
    hidden,
    cot,
    inputs,
    param_hbm,
    noise_hbm,
    outputs,
    new_param,
    param,
    noise,
    far_hidden,
    far_cot,
    own,
    sib_out,
    sib_in,
    first,
    part,
    fresh,
    mix_out,
    mix_in,
    load_sem,
    hid_sem,
    cot_sem,
    sib_sem,
    part_sem,
    gather_sem,
    share_sem,
    mix_sem,
):
    seqs, span = inputs.shape[0], inputs.shape[1]
    width, outs = inputs.shape[2], param.shape[1]
    half = width // 2
    rows = outs // ring
    mine = rows // 2
    depth = ring // 2
    seq, fs = lax.axis_index("seq"), lax.axis_index("fsdp")
    core, y, z = seq % 2, (seq // 2) % 2, seq // 4
    p = z * (1 - y) + (ring - 1 - z) * y

    def device(position):
        low = jnp.where(position < depth, 0, 1)
        zz = jnp.where(position < depth, position, ring - 1 - position)
        return {"seq": (zz * 2 + low) * 2 + core}

    right, left = device((p + 1) % ring), device((p + ring - 1) % ring)
    sibling = {"seq": seq + 1 - 2 * core}
    far = {"fsdp": 1 - fs}

    param_load = pltpu.make_async_copy(param_hbm, param, load_sem.at[0])
    own_rows = p * rows + core * mine
    noise_load = pltpu.make_async_copy(
        noise_hbm.at[:, pl.ds(own_rows, mine), :], noise, load_sem.at[1]
    )
    param_load.start()
    noise_load.start()

    barrier = pltpu.get_barrier_semaphore()
    for other in (right, left, sibling, far):
        pl.semaphore_signal(barrier, inc=1, device_id=other, device_id_type=MESH)
    pl.semaphore_wait(barrier, 4)

    def remote(src, dst, sems, index, to):
        return pltpu.make_async_remote_copy(
            src_ref=src,
            dst_ref=dst,
            send_sem=sems.at[(0,) + index],
            recv_sem=sems.at[(1,) + index],
            device_id=to,
            device_id_type=MESH,
        )

    def chunk(j):
        m = j // 2 + 1
        offset = jnp.where(j % 2 == 0, ring - m, m)
        return (p + jnp.where(j == ring - 1, 0, offset)) % ring

    hid_copy = remote(hidden, far_hidden, hid_sem, (0,), far)
    hid_copy.start()

    def cot_copy(j):
        q = chunk(j)
        return remote(
            cot.at[pl.ds((1 - fs) * outs + q * rows, rows), :],
            far_cot.at[pl.ds(q * rows, rows), :],
            cot_sem,
            (j,),
            far,
        )

    for j in range(ring):
        cot_copy(j).start()

    def forward(source, emit):
        tile = 256
        tiles = outs // tile

        def body(i, carry):
            b, o = i // tiles, pl.multiple_of((i % tiles) * tile, tile)
            total = jnp.zeros((span, tile), F32)
            for tap in range(3):
                total += lax.dot_general(
                    source[b, tap * DILATION_STEP : tap * DILATION_STEP + span, :],
                    param[tap, pl.ds(o, tile), :],
                    (((1,), (1,)), ((), ())),
                    preferred_element_type=F32,
                )
            emit(b, o, tile, total * scale)
            return carry

        lax.fori_loop(0, seqs * tiles, body, 0)

    def emit_near(b, o, tile, value):
        at = pl.ds(pl.multiple_of(fs * outs + o, 128), tile)
        outputs[b, :, at] = (inputs[b, :, at].astype(F32) + value).astype(BF16)

    def emit_far(b, o, tile, value):
        mix_out[b, :, pl.ds(o, tile)] = value.astype(BF16)

    param_load.wait()
    forward(hidden, emit_near)
    hid_copy.wait_recv()

    def sib_copy(j):
        q = chunk(j)
        return remote(sib_out.at[q], sib_in.at[q], sib_sem, (j,), sibling)

    def grads(first_stage):
        for j in (first_stage, first_stage + 1):
            cot_copy(j).wait_recv()

        def body(i, carry):
            q = chunk(first_stage + i)
            for tap in range(3):
                total = jnp.zeros((rows, width), F32)
                for b in range(seqs):
                    at = slice(tap * DILATION_STEP, tap * DILATION_STEP + span)
                    near_row = fs * outs + q * rows
                    columns = slice(b * span, (b + 1) * span)
                    total += jnp.dot(
                        cot[pl.ds(near_row, rows), columns],
                        hidden[b, at, :],
                        preferred_element_type=F32,
                    )
                    total += jnp.dot(
                        far_cot[pl.ds(q * rows, rows), columns],
                        far_hidden[b, at, :],
                        preferred_element_type=F32,
                    )
                total = total * scale
                low, high = total[:mine], total[mine:]
                own[q, tap] = jnp.where(core == 0, low, high)
                sib_out[q, tap] = jnp.where(core == 0, high, low).astype(BF16)
            return carry

        lax.fori_loop(0, 2, body, 0)
        for j in (first_stage, first_stage + 1):
            sib_copy(j).start()
        for j in (first_stage, first_stage + 1):
            sib_copy(j).wait_recv()
            q = chunk(j)
            for tap in range(3):
                own[q, tap] += sib_in[q, tap].astype(F32)

    def columns(d):
        return slice(d * half, (d + 1) * half)

    def behind(d, count):
        return (p + (ring - count if d == 0 else count)) % ring

    grads(0)
    for d in range(2):
        for tap in range(3):
            first[d, tap] = own[behind(d, 1), tap, :, columns(d)].astype(BF16)

    def part_copy(d, s):
        source = first.at[d] if s == 0 else part.at[d, s - 1]
        return remote(source, part.at[d, s], part_sem, (d, s), (right, left)[d])

    mix_copy = remote(mix_out, mix_in, mix_sem, (0,), far)
    for s in range(ring - 1):
        for d in range(2):
            part_copy(d, s).start()
        if 2 * s + 2 < ring:
            grads(2 * s + 2)
        elif 2 * s == ring:
            forward(far_hidden, emit_far)
            mix_copy.start()
        for d in range(2):
            part_copy(d, s).wait_recv()
            if s < ring - 2:
                q = behind(d, s + 2)
                for tap in range(3):
                    value = part[d, s, tap].astype(F32) + own[q, tap, :, columns(d)]
                    part[d, s, tap] = value.astype(BF16)

    noise_load.wait()
    for d in range(2):
        for tap in range(3):
            at = columns(d)
            grad = part[d, ring - 2, tap].astype(F32) + own[p, tap, :, at]
            fresh[tap, :, at] = (
                param[tap, pl.ds(own_rows, mine), at].astype(F32)
                - eta * grad
                + math.sqrt(2.0 * eta) * noise[tap, :, at].astype(F32)
            ).astype(BF16)

    def place(q, at):
        return new_param.at[:, pl.ds(q * rows + core * mine, mine), at]

    def gather_copy(d, s):
        spot = place(behind(d, s) if s else p, columns(d))
        source = fresh.at[:, :, columns(d)] if s == 0 else spot
        return remote(source, spot, gather_sem, (d, s), (right, left)[d])

    def share_copy(d, s):
        spot = place(behind(d, s) if s else p, columns(d))
        source = fresh.at[:, :, columns(d)] if s == 0 else spot
        return remote(source, spot, share_sem, (d, s), sibling)

    keep = pltpu.make_async_copy(fresh, place(p, slice(0, width)), load_sem.at[2])
    for d in range(2):
        gather_copy(d, 0).start()
    keep.start()
    for d in range(2):
        share_copy(d, 0).start()
    for s in range(ring - 1):
        if s == ring - 2:
            mix_copy.wait_recv()
            at = pl.ds(pl.multiple_of((1 - fs) * outs, 128), outs)
            for b in range(seqs):
                outputs[b, :, at] = (
                    inputs[b, :, at].astype(F32) + mix_in[b].astype(F32)
                ).astype(BF16)
        for d in range(2):
            gather_copy(d, s).wait_recv()
            if s < ring - 2:
                gather_copy(d, s + 1).start()
            share_copy(d, s + 1).start()

    for d in range(2):
        for s in range(ring):
            share_copy(d, s).wait()
        for s in range(ring - 1):
            gather_copy(d, s).wait_send()
            part_copy(d, s).wait_send()
    for j in range(ring):
        cot_copy(j).wait_send()
        sib_copy(j).wait_send()
    hid_copy.wait_send()
    mix_copy.wait_send()
    keep.wait()


def ring_step(inputs, gain, param, cotangent, noise):
    seqs, span, width = inputs.shape
    outs = param.shape[0]
    ring = lax.axis_size("seq") // 2
    scale = 1.0 / math.sqrt(3.0 * width)
    total_rows = seqs * lax.axis_size("fsdp") * span * lax.axis_size("seq")
    eta = math.sqrt(3.0 * width / total_rows)
    hidden = padded(normalise(inputs, gain), (("seq", 1),), DILATION_STEP)
    cot = jnp.transpose(cotangent, (2, 0, 1)).reshape(width, seqs * span)
    mine = outs // ring // 2
    vmem, anywhere = (pl.BlockSpec(memory_space=pltpu.VMEM), pl.BlockSpec(memory_space=pl.ANY))
    dma = pltpu.SemaphoreType.DMA
    flops = 4 * 3 * 2 * seqs * span * width * outs
    outputs, new_param = pl.pallas_call(
        functools.partial(ring_kernel, ring, scale, eta),
        out_shape=(
            jax.ShapeDtypeStruct(inputs.shape, BF16),
            jax.ShapeDtypeStruct((3, outs, width), BF16),
        ),
        in_specs=[vmem, vmem, vmem, anywhere, anywhere],
        out_specs=(vmem, anywhere),
        scratch_shapes=[
            pltpu.VMEM((3, outs, width), BF16),
            pltpu.VMEM((3, mine, width), BF16),
            pltpu.VMEM(hidden.shape, BF16),
            pltpu.VMEM((outs, seqs * span), BF16),
            pltpu.VMEM((ring, 3, mine, width), F32),
            pltpu.VMEM((ring, 3, mine, width), BF16),
            pltpu.VMEM((ring, 3, mine, width), BF16),
            pltpu.VMEM((2, 3, mine, width // 2), BF16),
            pltpu.VMEM((2, ring - 1, 3, mine, width // 2), BF16),
            pltpu.VMEM((3, mine, width), BF16),
            pltpu.VMEM((seqs, span, outs), BF16),
            pltpu.VMEM((seqs, span, outs), BF16),
            dma((3,)),
            dma((2, 1)),
            dma((2, ring)),
            dma((2, ring)),
            dma((2, 2, ring - 1)),
            dma((2, 2, ring - 1)),
            dma((2, 2, ring)),
            dma((2, 1)),
        ],
        compiler_params=pltpu.CompilerParams(
            collective_id=0, has_side_effects=True, vmem_limit_bytes=60 * 2**20
        ),
        cost_estimate=pl.CostEstimate(
            flops=flops, bytes_accessed=30 * 2**20, transcendentals=0
        ),
    )(
        hidden,
        cot,
        inputs,
        jnp.transpose(param, (1, 0, 2)),
        jnp.transpose(noise, (1, 0, 2)),
    )
    return (outputs, jnp.transpose(new_param, (1, 0, 2)))


def fits(mesh):
    seq, fsdp = mesh.shape["seq"], mesh.shape["fsdp"]

    def step(inputs, gain, param, cotangent, noise):
        seqs, span, width = inputs.shape
        outs = param.shape[0]
        ok = fsdp == 2 and seq % 8 == 0 and outs % (16 * seq) == 0
        ok = ok and span % 128 == 0 and width % 256 == 0 and outs % 256 == 0
        return (ring_step if ok else shards)(inputs, gain, param, cotangent, noise)

    return step


def solution(mesh):
    placed = (
        P("fsdp", "seq", None),
        P(),
        P("fsdp", None, None),
        P("fsdp", "seq", None),
        P("fsdp", None, None),
    )
    return jax.shard_map(
        fits(mesh),
        mesh=mesh,
        in_specs=placed,
        out_specs=(P("fsdp", "seq", None), P("fsdp", None, None)),
        check_vma=False,
    )
```

```python
import functools
import math

import jax
import jax.numpy as jnp
from jax import lax
from jax.experimental import pallas as pl
from jax.experimental.pallas import tpu as pltpu
from jax.sharding import PartitionSpec as P

DILATION_STEP = 16
MESH = pl.DeviceIdType.MESH
F32 = jnp.float32
BF16 = jnp.bfloat16


def padded(x, sides, width):
    for axis, dim in sides:
        count, length = (lax.axis_size(axis), x.shape[dim])
        up = [(i, (i + 1) % count) for i in range(count - 1)]
        down = [(j, i) for i, j in up]
        last = lax.slice_in_dim(x, length - width, length, axis=dim)
        first = lax.slice_in_dim(x, 0, width, axis=dim)
        before = lax.ppermute(last, axis, up)
        after = lax.ppermute(first, axis, down)
        x = jnp.concatenate([before, x, after], axis=dim)
    return x


def normalise(values, gain):
    floats = values.astype(jnp.float32)
    factor = lax.rsqrt(jnp.mean(floats * floats, axis=-1, keepdims=True) + 1e-06)
    return jax.nn.gelu(floats * factor * gain).astype(jnp.bfloat16)


def convolve(source_rows, kernel, scale):
    span_length = source_rows.shape[1] - 2 * DILATION_STEP
    total = jnp.zeros((source_rows.shape[0], span_length, kernel.shape[0]), jnp.float32)
    for kernel_tap in range(3):
        input_window = source_rows[
            :, kernel_tap * DILATION_STEP : kernel_tap * DILATION_STEP + span_length, :
        ]
        total = total + lax.dot_general(
            input_window,
            kernel[:, kernel_tap, :],
            (((2,), (1,)), ((), ())),
            preferred_element_type=jnp.float32,
        )
    return total * scale


def shards(inputs, gain, param, cotangent, noise):
    seqs, span_length, width = inputs.shape
    scale = 1.0 / math.sqrt(3.0 * width)
    total_rows = seqs * lax.axis_size("fsdp") * span_length * lax.axis_size("seq")
    eta = math.sqrt(3.0 * width / total_rows)
    hidden_state = normalise(inputs, gain)
    padded_input = padded(hidden_state, (("seq", 1),), DILATION_STEP)
    mixed = convolve(padded_input, lax.all_gather(param, "fsdp", axis=0, tiled=True), scale)
    taps = []
    for kernel_tap in range(3):
        input_window = padded_input[
            :, kernel_tap * DILATION_STEP : kernel_tap * DILATION_STEP + span_length, :
        ]
        taps.append(
            lax.dot_general(
                cotangent,
                input_window,
                (((0, 1), (0, 1)), ((), ())),
                preferred_element_type=jnp.float32,
            )
        )
    term = (jnp.stack(taps, axis=1) * scale).astype(jnp.bfloat16)
    term = lax.optimization_barrier(term)
    share = lax.psum_scatter(
        term.astype(jnp.float32).astype(jnp.bfloat16), "fsdp", scatter_dimension=0, tiled=True
    ).astype(jnp.float32)
    seq_share = lax.psum_scatter(share, "seq", scatter_dimension=0, tiled=True)
    piece_rows = seq_share.shape[0]
    offset = lax.axis_index("seq") * piece_rows
    own_param = lax.dynamic_slice_in_dim(param, offset, piece_rows, 0)
    own_noise = lax.dynamic_slice_in_dim(noise, offset, piece_rows, 0)
    updated = (
        own_param.astype(jnp.float32)
        - eta * seq_share
        + math.sqrt(2.0 * eta) * own_noise.astype(jnp.float32)
    )
    new_param = lax.all_gather(updated.astype(jnp.bfloat16), "seq", axis=0, tiled=True)
    outputs = (inputs.astype(jnp.float32) + mixed).astype(jnp.bfloat16)
    return (outputs, new_param)


def ring_kernel(
    ring,
    scale,
    eta,
    hidden,
    cot,
    inputs,
    param_hbm,
    noise_hbm,
    outputs,
    new_param,
    param,
    noise,
    far_hidden,
    far_cot,
    near,
    sib_out,
    sib_in,
    first,
    part,
    fresh,
    mix_out,
    mix_in,
    load_sem,
    hid_sem,
    cot_sem,
    sib_sem,
    part_sem,
    gather_sem,
    share_sem,
    mix_sem,
):
    seqs, span = inputs.shape[0], inputs.shape[1]
    width, outs = inputs.shape[2], param.shape[1]
    half = width // 2
    rows = outs // ring
    mine = rows // 2
    depth = ring // 2
    seq, fs = lax.axis_index("seq"), lax.axis_index("fsdp")
    core, y, z = seq % 2, (seq // 2) % 2, seq // 4
    p = z * (1 - y) + (ring - 1 - z) * y

    def device(position):
        low = jnp.where(position < depth, 0, 1)
        zz = jnp.where(position < depth, position, ring - 1 - position)
        return {"seq": (zz * 2 + low) * 2 + core}

    right, left = device((p + 1) % ring), device((p + ring - 1) % ring)
    sibling = {"seq": seq + 1 - 2 * core}
    far = {"fsdp": 1 - fs}

    param_load = pltpu.make_async_copy(param_hbm, param, load_sem.at[0])
    own_rows = p * rows + core * mine
    noise_load = pltpu.make_async_copy(
        noise_hbm.at[:, pl.ds(own_rows, mine), :], noise, load_sem.at[1]
    )
    param_load.start()
    noise_load.start()

    barrier = pltpu.get_barrier_semaphore()
    for other in (right, left, sibling, far):
        pl.semaphore_signal(barrier, inc=1, device_id=other, device_id_type=MESH)
    pl.semaphore_wait(barrier, 4)

    def remote(src, dst, sems, index, to):
        return pltpu.make_async_remote_copy(
            src_ref=src,
            dst_ref=dst,
            send_sem=sems.at[(0,) + index],
            recv_sem=sems.at[(1,) + index],
            device_id=to,
            device_id_type=MESH,
        )

    def chunk(j):
        m = j // 2 + 1
        offset = jnp.where(j % 2 == 0, ring - m, m)
        return (p + jnp.where(j == ring - 1, 0, offset)) % ring

    hid_copy = remote(hidden, far_hidden, hid_sem, (0,), far)
    hid_copy.start()

    def cot_copy(j):
        q = chunk(j)
        return remote(
            cot.at[pl.ds((1 - fs) * outs + q * rows, rows), :],
            far_cot.at[pl.ds(q * rows, rows), :],
            cot_sem,
            (j,),
            far,
        )

    for j in range(ring):
        cot_copy(j).start()

    tile = 256
    tiles = outs // tile

    def forward(source, emit, start, stop):
        def body(i, carry):
            b, o = i // tiles, pl.multiple_of((i % tiles) * tile, tile)
            total = jnp.zeros((span, tile), F32)
            for tap in range(3):
                total += lax.dot_general(
                    source[b, tap * DILATION_STEP : tap * DILATION_STEP + span, :],
                    param[tap, pl.ds(o, tile), :],
                    (((1,), (1,)), ((), ())),
                    preferred_element_type=F32,
                )
            emit(b, o, tile, total * scale)
            return carry

        lax.fori_loop(start, stop, body, 0)

    def emit_near(b, o, tile, value):
        at = pl.ds(pl.multiple_of(fs * outs + o, 128), tile)
        outputs[b, :, at] = (inputs[b, :, at].astype(F32) + value).astype(BF16)

    def emit_far(b, o, tile, value):
        mix_out[b, :, pl.ds(o, tile)] = value.astype(BF16)

    def window(tap):
        return slice(tap * DILATION_STEP, tap * DILATION_STEP + span)

    def near_grads(i, carry):
        o = pl.multiple_of(i * tile, tile)
        for tap in range(3):
            total = jnp.zeros((tile, width), F32)
            for b in range(seqs):
                total += jnp.dot(
                    cot[pl.ds(fs * outs + o, tile), b * span : (b + 1) * span],
                    hidden[b, window(tap), :],
                    preferred_element_type=F32,
                )
            near[tap, pl.ds(o, tile), :] = total * scale
        return carry

    lax.fori_loop(0, tiles, near_grads, 0)
    param_load.wait()
    forward(hidden, emit_near, 0, seqs * tiles)
    hid_copy.wait_recv()

    def sib_copy(j):
        q = chunk(j)
        return remote(sib_out.at[q], sib_in.at[q], sib_sem, (j,), sibling)

    def grads(first_stage):
        for i in range(2):
            j = first_stage + i
            cot_copy(j).wait_recv()
            q = chunk(j)
            chunk_rows = pl.ds(q * rows, rows)
            for tap in range(3):
                total = jnp.zeros((rows, width), F32)
                for b in range(seqs):
                    total += jnp.dot(
                        far_cot[chunk_rows, b * span : (b + 1) * span],
                        far_hidden[b, window(tap), :],
                        preferred_element_type=F32,
                    )
                total = total * scale + near[tap, chunk_rows, :]
                near[tap, chunk_rows, :] = total
                low, high = total[:mine], total[mine:]
                sib_out[q, tap] = jnp.where(core == 0, high, low).astype(BF16)
            sib_copy(j).start()

    def columns(d):
        return slice(d * half, (d + 1) * half)

    def behind(d, count):
        return (p + (ring - count if d == 0 else count)) % ring

    def own(q, tap, d):
        at = near[tap, pl.ds(q * rows + core * mine, mine), columns(d)]
        return at + sib_in[q, tap, :, columns(d)].astype(F32)

    def part_copy(d, s, tap):
        source = first.at[d, tap] if s == 0 else part.at[d, s - 1, tap]
        to = (right, left)[d]
        return remote(source, part.at[d, s, tap], part_sem, (d, s, tap), to)

    def place(q, tap, at):
        return new_param.at[tap, pl.ds(q * rows + core * mine, mine), at]

    def gather_copy(d, s, tap):
        spot = place(behind(d, s), tap, columns(d))
        source = fresh.at[tap, :, columns(d)] if s == 0 else spot
        return remote(source, spot, gather_sem, (d, s, tap), (right, left)[d])

    def share_copy(d, s):
        q = behind(d, s)
        spot = new_param.at[:, pl.ds(q * rows + core * mine, mine), columns(d)]
        source = fresh.at[:, :, columns(d)] if s == 0 else spot
        return remote(source, spot, share_sem, (d, s), sibling)

    grads(0)
    for j in range(2):
        sib_copy(j).wait_recv()
    for tap in range(3):
        for d in range(2):
            first[d, tap] = own(behind(d, 1), tap, d).astype(BF16)
            part_copy(d, 0, tap).start()

    mix_copy = remote(mix_out, mix_in, mix_sem, (0,), far)
    stages = ring // 2 - 1
    spread = ring - 2 - stages
    pieces = seqs * tiles
    for s in range(ring - 1):
        if s < stages:
            grads(2 * s + 2)
            for j in range(2):
                sib_copy(2 * s + 2 + j).wait_recv()
        elif s < ring - 2:
            at = s - stages
            forward(
                far_hidden, emit_far, at * pieces // spread, (at + 1) * pieces // spread
            )
            if at == spread - 1:
                mix_copy.start()
        else:
            noise_load.wait()
        for tap in range(3):
            for d in range(2):
                part_copy(d, s, tap).wait_recv()
                total = part[d, s, tap].astype(F32) + own(behind(d, s + 2), tap, d)
                if s < ring - 2:
                    part[d, s, tap] = total.astype(BF16)
                    part_copy(d, s + 1, tap).start()
                else:
                    at = columns(d)
                    fresh[tap, :, at] = (
                        param[tap, pl.ds(own_rows, mine), at].astype(F32)
                        - eta * total
                        + math.sqrt(2.0 * eta) * noise[tap, :, at].astype(F32)
                    ).astype(BF16)
                    gather_copy(d, 0, tap).start()

    keep = pltpu.make_async_copy(
        fresh, new_param.at[:, pl.ds(own_rows, mine), :], load_sem.at[2]
    )
    keep.start()
    for d in range(2):
        share_copy(d, 0).start()
    for s in range(ring - 1):
        if s == ring - 3:
            mix_copy.wait_recv()
            at = pl.ds(pl.multiple_of((1 - fs) * outs, 128), outs)
            for b in range(seqs):
                outputs[b, :, at] = (
                    inputs[b, :, at].astype(F32) + mix_in[b].astype(F32)
                ).astype(BF16)
        for tap in range(3):
            for d in range(2):
                gather_copy(d, s, tap).wait_recv()
                if s < ring - 2:
                    gather_copy(d, s + 1, tap).start()
        for d in range(2):
            share_copy(d, s + 1).start()

    for d in range(2):
        for s in range(ring):
            share_copy(d, s).wait()
        for s in range(ring - 1):
            for tap in range(3):
                gather_copy(d, s, tap).wait_send()
                part_copy(d, s, tap).wait_send()
    for j in range(ring):
        cot_copy(j).wait_send()
        sib_copy(j).wait_send()
    hid_copy.wait_send()
    mix_copy.wait_send()
    keep.wait()


def ring_step(inputs, gain, param, cotangent, noise):
    seqs, span, width = inputs.shape
    outs = param.shape[0]
    ring = lax.axis_size("seq") // 2
    scale = 1.0 / math.sqrt(3.0 * width)
    total_rows = seqs * lax.axis_size("fsdp") * span * lax.axis_size("seq")
    eta = math.sqrt(3.0 * width / total_rows)
    hidden = padded(normalise(inputs, gain), (("seq", 1),), DILATION_STEP)
    cot = jnp.transpose(cotangent, (2, 0, 1)).reshape(width, seqs * span)
    mine = outs // ring // 2
    vmem, anywhere = (pl.BlockSpec(memory_space=pltpu.VMEM), pl.BlockSpec(memory_space=pl.ANY))
    dma = pltpu.SemaphoreType.DMA
    flops = 4 * 3 * 2 * seqs * span * width * outs
    outputs, new_param = pl.pallas_call(
        functools.partial(ring_kernel, ring, scale, eta),
        out_shape=(
            jax.ShapeDtypeStruct(inputs.shape, BF16),
            jax.ShapeDtypeStruct((3, outs, width), BF16),
        ),
        in_specs=[vmem, vmem, vmem, anywhere, anywhere],
        out_specs=(vmem, anywhere),
        scratch_shapes=[
            pltpu.VMEM((3, outs, width), BF16),
            pltpu.VMEM((3, mine, width), BF16),
            pltpu.VMEM(hidden.shape, BF16),
            pltpu.VMEM((outs, seqs * span), BF16),
            pltpu.VMEM((3, outs, width), F32),
            pltpu.VMEM((ring, 3, mine, width), BF16),
            pltpu.VMEM((ring, 3, mine, width), BF16),
            pltpu.VMEM((2, 3, mine, width // 2), BF16),
            pltpu.VMEM((2, ring - 1, 3, mine, width // 2), BF16),
            pltpu.VMEM((3, mine, width), BF16),
            pltpu.VMEM((seqs, span, outs), BF16),
            pltpu.VMEM((seqs, span, outs), BF16),
            dma((3,)),
            dma((2, 1)),
            dma((2, ring)),
            dma((2, ring)),
            dma((2, 2, ring - 1, 3)),
            dma((2, 2, ring - 1, 3)),
            dma((2, 2, ring)),
            dma((2, 1)),
        ],
        compiler_params=pltpu.CompilerParams(
            collective_id=0, has_side_effects=True, vmem_limit_bytes=50 * 2**20
        ),
        cost_estimate=pl.CostEstimate(
            flops=flops, bytes_accessed=30 * 2**20, transcendentals=0
        ),
    )(
        hidden,
        cot,
        inputs,
        jnp.transpose(param, (1, 0, 2)),
        jnp.transpose(noise, (1, 0, 2)),
    )
    return (outputs, jnp.transpose(new_param, (1, 0, 2)))


def fits(mesh):
    seq, fsdp = mesh.shape["seq"], mesh.shape["fsdp"]

    def step(inputs, gain, param, cotangent, noise):
        seqs, span, width = inputs.shape
        outs = param.shape[0]
        ok = fsdp == 2 and seq % 8 == 0 and outs % (16 * seq) == 0
        ok = ok and span % 128 == 0 and width % 256 == 0 and outs % 256 == 0
        return (ring_step if ok else shards)(inputs, gain, param, cotangent, noise)

    return step


def solution(mesh):
    placed = (
        P("fsdp", "seq", None),
        P(),
        P("fsdp", None, None),
        P("fsdp", "seq", None),
        P("fsdp", None, None),
    )
    return jax.shard_map(
        fits(mesh),
        mesh=mesh,
        in_specs=placed,
        out_specs=(P("fsdp", "seq", None), P("fsdp", None, None)),
        check_vma=False,
    )
```

```python
import functools
import math

import jax
import jax.numpy as jnp
from jax import lax
from jax.experimental import pallas as pl
from jax.experimental.pallas import tpu as pltpu
from jax.sharding import PartitionSpec as P

DILATION_STEP = 16
MESH = pl.DeviceIdType.MESH
F32 = jnp.float32
BF16 = jnp.bfloat16


def padded(x, sides, width):
    for axis, dim in sides:
        count, length = (lax.axis_size(axis), x.shape[dim])
        up = [(i, (i + 1) % count) for i in range(count - 1)]
        down = [(j, i) for i, j in up]
        last = lax.slice_in_dim(x, length - width, length, axis=dim)
        first = lax.slice_in_dim(x, 0, width, axis=dim)
        before = lax.ppermute(last, axis, up)
        after = lax.ppermute(first, axis, down)
        x = jnp.concatenate([before, x, after], axis=dim)
    return x


def normalise(values, gain):
    floats = values.astype(jnp.float32)
    factor = lax.rsqrt(jnp.mean(floats * floats, axis=-1, keepdims=True) + 1e-06)
    return jax.nn.gelu(floats * factor * gain).astype(jnp.bfloat16)


def convolve(source_rows, kernel, scale):
    span_length = source_rows.shape[1] - 2 * DILATION_STEP
    total = jnp.zeros((source_rows.shape[0], span_length, kernel.shape[0]), jnp.float32)
    for kernel_tap in range(3):
        input_window = source_rows[
            :, kernel_tap * DILATION_STEP : kernel_tap * DILATION_STEP + span_length, :
        ]
        total = total + lax.dot_general(
            input_window,
            kernel[:, kernel_tap, :],
            (((2,), (1,)), ((), ())),
            preferred_element_type=jnp.float32,
        )
    return total * scale


def shards(inputs, gain, param, cotangent, noise):
    seqs, span_length, width = inputs.shape
    scale = 1.0 / math.sqrt(3.0 * width)
    total_rows = seqs * lax.axis_size("fsdp") * span_length * lax.axis_size("seq")
    eta = math.sqrt(3.0 * width / total_rows)
    hidden_state = normalise(inputs, gain)
    padded_input = padded(hidden_state, (("seq", 1),), DILATION_STEP)
    mixed = convolve(padded_input, lax.all_gather(param, "fsdp", axis=0, tiled=True), scale)
    taps = []
    for kernel_tap in range(3):
        input_window = padded_input[
            :, kernel_tap * DILATION_STEP : kernel_tap * DILATION_STEP + span_length, :
        ]
        taps.append(
            lax.dot_general(
                cotangent,
                input_window,
                (((0, 1), (0, 1)), ((), ())),
                preferred_element_type=jnp.float32,
            )
        )
    term = (jnp.stack(taps, axis=1) * scale).astype(jnp.bfloat16)
    term = lax.optimization_barrier(term)
    share = lax.psum_scatter(
        term.astype(jnp.float32).astype(jnp.bfloat16), "fsdp", scatter_dimension=0, tiled=True
    ).astype(jnp.float32)
    seq_share = lax.psum_scatter(share, "seq", scatter_dimension=0, tiled=True)
    piece_rows = seq_share.shape[0]
    offset = lax.axis_index("seq") * piece_rows
    own_param = lax.dynamic_slice_in_dim(param, offset, piece_rows, 0)
    own_noise = lax.dynamic_slice_in_dim(noise, offset, piece_rows, 0)
    updated = (
        own_param.astype(jnp.float32)
        - eta * seq_share
        + math.sqrt(2.0 * eta) * own_noise.astype(jnp.float32)
    )
    new_param = lax.all_gather(updated.astype(jnp.bfloat16), "seq", axis=0, tiled=True)
    outputs = (inputs.astype(jnp.float32) + mixed).astype(jnp.bfloat16)
    return (outputs, new_param)


def ring_kernel(
    ring,
    scale,
    eta,
    body_hidden,
    cot,
    inputs,
    param_hbm,
    noise_hbm,
    outputs,
    new_param,
    param,
    noise,
    hidden,
    far_hidden,
    far_cot,
    near,
    sib_out,
    sib_in,
    first,
    part,
    fresh,
    mix_out,
    mix_in,
    load_sem,
    edge_sem,
    hid_sem,
    cot_sem,
    sib_sem,
    part_sem,
    gather_sem,
    share_sem,
    mix_sem,
):
    seqs, span = inputs.shape[0], inputs.shape[1]
    width, outs = inputs.shape[2], param.shape[1]
    half = width // 2
    rows = outs // ring
    mine = rows // 2
    depth = ring // 2
    seq, fs = lax.axis_index("seq"), lax.axis_index("fsdp")
    core, y, z = seq % 2, (seq // 2) % 2, seq // 4
    p = z * (1 - y) + (ring - 1 - z) * y

    def device(position):
        low = jnp.where(position < depth, 0, 1)
        zz = jnp.where(position < depth, position, ring - 1 - position)
        return {"seq": (zz * 2 + low) * 2 + core}

    right, left = device((p + 1) % ring), device((p + ring - 1) % ring)
    sibling = {"seq": seq + 1 - 2 * core}
    far = {"fsdp": 1 - fs}

    param_load = pltpu.make_async_copy(param_hbm, param, load_sem.at[0])
    own_rows = p * rows + core * mine
    noise_load = pltpu.make_async_copy(
        noise_hbm.at[:, pl.ds(own_rows, mine), :], noise, load_sem.at[1]
    )
    param_load.start()
    noise_load.start()

    barrier = pltpu.get_barrier_semaphore()
    for other in (right, left, far):
        pl.semaphore_signal(barrier, inc=1, device_id=other, device_id_type=MESH)
    has_before, has_after = seq > 0, seq < 2 * ring - 1
    before, after = {"seq": seq - 1}, {"seq": seq + 1}
    for there, other in ((has_before, before), (has_after, after)):

        @pl.when(there)
        def _():
            pl.semaphore_signal(barrier, inc=1, device_id=other, device_id_type=MESH)

    edges = jnp.where(has_before, 1, 0) + jnp.where(has_after, 1, 0)
    pl.semaphore_wait(barrier, 3 + edges)

    def remote(src, dst, sems, index, to):
        return pltpu.make_async_remote_copy(
            src_ref=src,
            dst_ref=dst,
            send_sem=sems.at[(0,) + index],
            recv_sem=sems.at[(1,) + index],
            device_id=to,
            device_id_type=MESH,
        )

    def chunk(j):
        m = j // 2 + 1
        offset = jnp.where(j % 2 == 0, ring - m, m)
        return (p + jnp.where(j == ring - 1, 0, offset)) % ring

    step = DILATION_STEP
    inner, head, tail = (slice(step, step + span), slice(0, step), slice(step + span, None))
    edge_up = remote(
        body_hidden.at[:, span - step :, :], hidden.at[:, head, :], edge_sem, (0,), after
    )
    edge_down = remote(
        body_hidden.at[:, :step, :], hidden.at[:, tail, :], edge_sem, (1,), before
    )
    pl.when(has_after)(edge_up.start)
    pl.when(has_before)(edge_down.start)
    hid_copy = remote(body_hidden, far_hidden.at[:, inner, :], hid_sem, (0,), far)
    hid_copy.start()
    inner_copy = pltpu.make_async_copy(body_hidden, hidden.at[:, inner, :], load_sem.at[3])
    inner_copy.start()
    for there, where in ((has_before, head), (has_after, tail)):

        @pl.when(jnp.logical_not(there))
        def _():
            hidden[:, where, :] = jnp.zeros((seqs, step, width), BF16)


    def cot_copy(j):
        q = chunk(j)
        return remote(
            cot.at[pl.ds((1 - fs) * outs + q * rows, rows), :],
            far_cot.at[pl.ds(q * rows, rows), :],
            cot_sem,
            (j,),
            far,
        )

    for j in range(ring):
        cot_copy(j).start()

    tile = 256
    tiles = outs // tile

    def forward(source, emit, start, stop):
        def body(i, carry):
            b, o = i // tiles, pl.multiple_of((i % tiles) * tile, tile)
            total = jnp.zeros((span, tile), F32)
            for tap in range(3):
                total += lax.dot_general(
                    source[b, tap * DILATION_STEP : tap * DILATION_STEP + span, :],
                    param[tap, pl.ds(o, tile), :],
                    (((1,), (1,)), ((), ())),
                    preferred_element_type=F32,
                )
            emit(b, o, tile, total * scale)
            return carry

        lax.fori_loop(start, stop, body, 0)

    def emit_near(b, o, tile, value):
        at = pl.ds(pl.multiple_of(fs * outs + o, 128), tile)
        outputs[b, :, at] = (inputs[b, :, at].astype(F32) + value).astype(BF16)

    def emit_far(b, o, tile, value):
        mix_out[b, :, pl.ds(o, tile)] = value.astype(BF16)

    def window(tap):
        return slice(tap * DILATION_STEP, tap * DILATION_STEP + span)

    def near_grads(i, carry):
        o = pl.multiple_of(i * tile, tile)
        for tap in range(3):
            total = jnp.zeros((tile, width), F32)
            for b in range(seqs):
                total += jnp.dot(
                    cot[pl.ds(fs * outs + o, tile), b * span : (b + 1) * span],
                    hidden[b, window(tap), :],
                    preferred_element_type=F32,
                )
            near[tap, pl.ds(o, tile), :] = total * scale
        return carry

    edge_head = remote(
        hidden.at[:, head, :], far_hidden.at[:, head, :], hid_sem, (1,), far
    )
    edge_tail = remote(
        hidden.at[:, tail, :], far_hidden.at[:, tail, :], hid_sem, (2,), far
    )
    pl.when(has_before)(edge_up.wait_recv)
    edge_head.start()
    pl.when(has_after)(edge_down.wait_recv)
    edge_tail.start()
    inner_copy.wait()
    lax.fori_loop(0, tiles, near_grads, 0)
    param_load.wait()
    forward(hidden, emit_near, 0, seqs * tiles)
    for copy in (hid_copy, edge_head, edge_tail):
        copy.wait_recv()

    def sib_copy(j):
        q = chunk(j)
        return remote(sib_out.at[q], sib_in.at[q], sib_sem, (j,), sibling)

    def grads(first_stage):
        for i in range(2):
            j = first_stage + i
            cot_copy(j).wait_recv()
            q = chunk(j)
            chunk_rows = pl.ds(q * rows, rows)
            for tap in range(3):
                total = jnp.zeros((rows, width), F32)
                for b in range(seqs):
                    total += jnp.dot(
                        far_cot[chunk_rows, b * span : (b + 1) * span],
                        far_hidden[b, window(tap), :],
                        preferred_element_type=F32,
                    )
                total = total * scale + near[tap, chunk_rows, :]
                near[tap, chunk_rows, :] = total
                low, high = total[:mine], total[mine:]
                sib_out[q, tap] = jnp.where(core == 0, high, low).astype(BF16)
            sib_copy(j).start()

    def columns(d):
        return slice(d * half, (d + 1) * half)

    def behind(d, count):
        return (p + (ring - count if d == 0 else count)) % ring

    def own(q, tap, d):
        at = near[tap, pl.ds(q * rows + core * mine, mine), columns(d)]
        return at + sib_in[q, tap, :, columns(d)].astype(F32)

    def part_copy(d, s, tap):
        source = first.at[d, tap] if s == 0 else part.at[d, s - 1, tap]
        to = (right, left)[d]
        return remote(source, part.at[d, s, tap], part_sem, (d, s, tap), to)

    def place(q, tap, at):
        return new_param.at[tap, pl.ds(q * rows + core * mine, mine), at]

    def gather_copy(d, s, tap):
        spot = place(behind(d, s), tap, columns(d))
        source = fresh.at[tap, :, columns(d)] if s == 0 else spot
        return remote(source, spot, gather_sem, (d, s, tap), (right, left)[d])

    def share_copy(d, s):
        q = behind(d, s)
        spot = new_param.at[:, pl.ds(q * rows + core * mine, mine), columns(d)]
        source = fresh.at[:, :, columns(d)] if s == 0 else spot
        return remote(source, spot, share_sem, (d, s), sibling)

    grads(0)
    for j in range(2):
        sib_copy(j).wait_recv()
    for tap in range(3):
        for d in range(2):
            first[d, tap] = own(behind(d, 1), tap, d).astype(BF16)
            part_copy(d, 0, tap).start()

    mix_copy = remote(mix_out, mix_in, mix_sem, (0,), far)
    stages = ring // 2 - 1
    spread = ring - 2 - stages
    pieces = seqs * tiles
    for s in range(ring - 1):
        if s < stages:
            grads(2 * s + 2)
            for j in range(2):
                sib_copy(2 * s + 2 + j).wait_recv()
        elif s < ring - 2:
            at = s - stages
            forward(
                far_hidden, emit_far, at * pieces // spread, (at + 1) * pieces // spread
            )
            if at == spread - 1:
                mix_copy.start()
        else:
            noise_load.wait()
        for tap in range(3):
            for d in range(2):
                part_copy(d, s, tap).wait_recv()
                total = part[d, s, tap].astype(F32) + own(behind(d, s + 2), tap, d)
                if s < ring - 2:
                    part[d, s, tap] = total.astype(BF16)
                    part_copy(d, s + 1, tap).start()
                else:
                    at = columns(d)
                    fresh[tap, :, at] = (
                        param[tap, pl.ds(own_rows, mine), at].astype(F32)
                        - eta * total
                        + math.sqrt(2.0 * eta) * noise[tap, :, at].astype(F32)
                    ).astype(BF16)
                    gather_copy(d, 0, tap).start()

    keep = pltpu.make_async_copy(
        fresh, new_param.at[:, pl.ds(own_rows, mine), :], load_sem.at[2]
    )
    keep.start()
    for d in range(2):
        share_copy(d, 0).start()
    for s in range(ring - 1):
        if s == ring - 3:
            mix_copy.wait_recv()
            at = pl.ds(pl.multiple_of((1 - fs) * outs, 128), outs)
            for b in range(seqs):
                outputs[b, :, at] = (
                    inputs[b, :, at].astype(F32) + mix_in[b].astype(F32)
                ).astype(BF16)
        for tap in range(3):
            for d in range(2):
                gather_copy(d, s, tap).wait_recv()
                if s < ring - 2:
                    gather_copy(d, s + 1, tap).start()
        for d in range(2):
            share_copy(d, s + 1).start()

    for d in range(2):
        for s in range(ring):
            share_copy(d, s).wait()
        for s in range(ring - 1):
            for tap in range(3):
                gather_copy(d, s, tap).wait_send()
                part_copy(d, s, tap).wait_send()
    for j in range(ring):
        cot_copy(j).wait_send()
        sib_copy(j).wait_send()
    for copy in (hid_copy, edge_head, edge_tail):
        copy.wait_send()
    pl.when(has_after)(edge_up.wait_send)
    pl.when(has_before)(edge_down.wait_send)
    mix_copy.wait_send()
    keep.wait()


def move_kernel(source, target, sems):
    taps, outs, _ = source.shape
    part = outs // 4
    copies = []
    for tap in range(taps):
        for i in range(4):
            at = (tap, slice(i * part, (i + 1) * part))
            copies.append(
                pltpu.make_async_copy(source.at[at], target.at[at], sems.at[tap, i])
            )
    for copy in copies:
        copy.start()
    for copy in copies:
        copy.wait()


def ring_step(inputs, gain, param, cotangent, noise):
    seqs, span, width = inputs.shape
    outs = param.shape[0]
    ring = lax.axis_size("seq") // 2
    scale = 1.0 / math.sqrt(3.0 * width)
    total_rows = seqs * lax.axis_size("fsdp") * span * lax.axis_size("seq")
    eta = math.sqrt(3.0 * width / total_rows)
    hidden = normalise(inputs, gain)
    wide = (seqs, span + 2 * DILATION_STEP, width)
    cot = jnp.transpose(cotangent, (2, 0, 1)).reshape(width, seqs * span)
    mine = outs // ring // 2
    vmem, anywhere = (pl.BlockSpec(memory_space=pltpu.VMEM), pl.BlockSpec(memory_space=pl.ANY))
    dma = pltpu.SemaphoreType.DMA
    flops = 4 * 3 * 2 * seqs * span * width * outs
    outputs, new_param = pl.pallas_call(
        functools.partial(ring_kernel, ring, scale, eta),
        out_shape=(
            jax.ShapeDtypeStruct(inputs.shape, BF16),
            jax.ShapeDtypeStruct((3, outs, width), BF16),
        ),
        in_specs=[vmem, vmem, vmem, anywhere, anywhere],
        out_specs=(vmem, anywhere),
        scratch_shapes=[
            pltpu.VMEM((3, outs, width), BF16),
            pltpu.VMEM((3, mine, width), BF16),
            pltpu.VMEM(wide, BF16),
            pltpu.VMEM(wide, BF16),
            pltpu.VMEM((outs, seqs * span), BF16),
            pltpu.VMEM((3, outs, width), F32),
            pltpu.VMEM((ring, 3, mine, width), BF16),
            pltpu.VMEM((ring, 3, mine, width), BF16),
            pltpu.VMEM((2, 3, mine, width // 2), BF16),
            pltpu.VMEM((2, ring - 1, 3, mine, width // 2), BF16),
            pltpu.VMEM((3, mine, width), BF16),
            pltpu.VMEM((seqs, span, outs), BF16),
            pltpu.VMEM((seqs, span, outs), BF16),
            dma((4,)),
            dma((2, 2)),
            dma((2, 3)),
            dma((2, ring)),
            dma((2, ring)),
            dma((2, 2, ring - 1, 3)),
            dma((2, 2, ring - 1, 3)),
            dma((2, 2, ring)),
            dma((2, 1)),
        ],
        compiler_params=pltpu.CompilerParams(
            collective_id=0, has_side_effects=True, vmem_limit_bytes=50 * 2**20
        ),
        cost_estimate=pl.CostEstimate(
            flops=flops, bytes_accessed=30 * 2**20, transcendentals=0
        ),
    )(
        hidden,
        cot,
        inputs,
        jnp.transpose(param, (1, 0, 2)),
        jnp.transpose(noise, (1, 0, 2)),
    )
    new_param = pl.pallas_call(
        move_kernel,
        out_shape=jax.ShapeDtypeStruct(new_param.shape, BF16),
        in_specs=[anywhere],
        out_specs=anywhere,
        scratch_shapes=[dma((3, 4))],
        cost_estimate=pl.CostEstimate(
            flops=0, bytes_accessed=2 * new_param.size * 2, transcendentals=0
        ),
    )(new_param)
    return (outputs, jnp.transpose(new_param, (1, 0, 2)))


def fits(mesh):
    seq, fsdp = mesh.shape["seq"], mesh.shape["fsdp"]

    def step(inputs, gain, param, cotangent, noise):
        seqs, span, width = inputs.shape
        outs = param.shape[0]
        ok = fsdp == 2 and seq % 8 == 0 and outs % (16 * seq) == 0
        ok = ok and span % 128 == 0 and width % 256 == 0 and outs % 256 == 0
        return (ring_step if ok else shards)(inputs, gain, param, cotangent, noise)

    return step


def solution(mesh):
    placed = (
        P("fsdp", "seq", None),
        P(),
        P("fsdp", None, None),
        P("fsdp", "seq", None),
        P("fsdp", None, None),
    )
    return jax.shard_map(
        fits(mesh),
        mesh=mesh,
        in_specs=placed,
        out_specs=(P("fsdp", "seq", None), P("fsdp", None, None)),
        check_vma=False,
    )
```
